32 devices in a mesh: shard: 8 (over y, x, core), seq: 4 (over z).
Axes of the slice: x: 2, y: 2, z: 4, core: 2. Of those that a mesh axis runs over, the one named last changes fastest.
Arguments:
- hidden_in: bfloat16 [16, 1024, 1024], P('shard', 'seq'), may hold values from -6 to 6
- condition: bfloat16 [16, 1024], P('shard'), may hold values from -6 to 6
- out_grad: bfloat16 [16, 1024, 1024], P('shard', 'seq'), may hold values from -6 to 6
- ada_weight: bfloat16 [1024, 6144], P(('shard', 'seq')), may hold values from -0.1875 to 0.1875
- qkv_weight: bfloat16 [1024, 3072], P(('shard', 'seq')), may hold values from -0.1875 to 0.1875
- proj_weight: bfloat16 [1024, 1024], P(('shard', 'seq')), may hold values from -1.5 to 1.5
- up_weight: bfloat16 [1024, 4096], P(('shard', 'seq')), may hold values from -0.1875 to 0.1875
- down_weight: bfloat16 [4096, 1024], P(('shard', 'seq')), may hold values from -0.09375 to 0.09375
- ada_bias: bfloat16 [6144], P(('shard', 'seq')), may hold values from -3 to 3
- qv_bias: bfloat16 [2048], P(('shard', 'seq')), may hold values from -3 to 3
- proj_bias: bfloat16 [1024], P(('shard', 'seq')), may hold values from -3 to 3
- up_bias: bfloat16 [4096], P(('shard', 'seq')), may hold values from -3 to 3
- down_bias: bfloat16 [1024], P(('shard', 'seq')), may hold values from -3 to 3
Outputs:
- block_out: bfloat16 [16, 1024, 1024], P('shard', 'seq')
- hidden_grad: float32 [16, 1024, 1024], P('shard', 'seq')
- condition_grad: float32 [16, 1024], P('shard')
- ada_grad: float32 [1024, 6144], P(('shard', 'seq'))
- qkv_grad: float32 [1024, 3072], P(('shard', 'seq'))
- proj_grad: float32 [1024, 1024], P(('shard', 'seq'))
- up_grad: float32 [1024, 4096], P(('shard', 'seq'))
- down_grad: float32 [4096, 1024], P(('shard', 'seq'))
- adabias_grad: float32 [6144], P(('shard', 'seq'))
- qvbias_grad: float32 [2048], P(('shard', 'seq'))
- projbias_grad: float32 [1024], P(('shard', 'seq'))
- upbias_grad: float32 [4096], P(('shard', 'seq'))
- downbias_grad: float32 [1024], P(('shard', 'seq'))
The draws below stay inside these ranges and needn't reach their ends.
All inputs are finite; a program needn't handle non-finite values.
Results may differ from the reference program's by a relative error of at most 0.013.
The reference program's roundings to bfloat16 on the way count: a program that leaves them out, or rounds other values in their place, can miss the bound.
Values may be sent and summed in bfloat16 or wider, within the bound.
No kernel may reach another device: no remote copies, remote signals or barrier semaphores. Data moves between devices by JAX's collectives and lax.ppermute only.
A program may use at most 256 MiB of HBM per device.

```python
import jax
import jax.numpy as jnp
from jax import lax

D = 1024
H = 16
HD = 64
FF = 4096
LENGTH = 1024
LATENTS = 16


def block_levels(own_key, shape, shards, smallest, high):
    def one(position, parts):
        draws = jax.random.uniform(jax.random.fold_in(jax.random.fold_in(own_key, 6), position), (parts,), jnp.float32, smallest / len(shards), high / len(shards))
        return jnp.repeat(jnp.exp(draws), shape[position] // parts).reshape((-1,) + (1,) * (len(shape) - position - 1))

    factor_of = one(*shards[0])
    for cut in shards[1:]:
        factor_of = factor_of * one(*cut)
    return factor_of


def centred(key, dims, spread, reach, split=(), held_as=jnp.bfloat16):
    gain = block_levels(key, dims, split, -0.22, 0.18) if split else 1.0
    array = jax.random.normal(key, dims, jnp.float32) * spread * gain
    return jnp.minimum(jnp.maximum(array, -reach), reach).astype(held_as)


def setup_inputs(seed: int = 0) -> dict:
    splits = jax.random.split(jax.random.key(seed), 14)
    return {
        "hidden_in": centred(splits[0], (LATENTS, LENGTH, D), 1.0, 6.0, ((0, 8), (1, 4))),
        "condition": centred(splits[1], (LATENTS, D), 1.0, 6.0, ((0, 8),)),
        "out_grad": centred(splits[2], (LATENTS, LENGTH, D), 1.0, 6.0, ((0, 8), (1, 4))),
        "ada_weight": centred(splits[3], (D, 6 * D), D ** -0.5, 0.1875, ((0, 32),)),
        "qkv_weight": centred(splits[4], (D, 3 * D), D ** -0.5, 0.1875, ((0, 32),)),
        "proj_weight": centred(splits[5], (D, D), (max(D * 16 // LENGTH, 1)) ** -0.5, 1.5, ((0, 32),)),
        "up_weight": centred(splits[6], (D, FF), D ** -0.5, 0.1875, ((0, 32),)),
        "down_weight": centred(splits[7], (FF, D), FF ** -0.5, 0.09375, ((0, 32),)),
        "ada_bias": centred(splits[8], (6 * D,), 0.5, 3.0, ((0, 32),)),
        "qv_bias": centred(splits[9], (2 * D,), 0.5, 3.0, ((0, 32),)),
        "proj_bias": centred(splits[10], (D,), 0.5, 3.0, ((0, 32),)),
        "up_bias": centred(splits[11], (FF,), 0.5, 3.0, ((0, 32),)),
        "down_bias": centred(splits[12], (D,), 0.5, 3.0, ((0, 32),)),
    }


EPS = 1e-06
PRECISE = lax.Precision.HIGHEST

@jax.custom_vjp
def low(v):
    return lax.optimization_barrier(v.astype(jnp.bfloat16)).astype(jnp.float32)

@jax.custom_vjp
def low_back(v):
    return v

def low_keep(v):
    return (low(v), None)

def low_pass(kept, grad):
    return (grad,)

def back_keep(v):
    return (v, None)

def back_low(kept, grad):
    return (low(grad),)
low.defvjp(low_keep, low_pass)
low_back.defvjp(back_keep, back_low)

def modulate(tokens, shift_by, scale_by):
    average = lax.optimization_barrier(jnp.mean(tokens, axis=-1, keepdims=True))
    centered = tokens - average
    variance = lax.optimization_barrier(jnp.mean(centered * centered, axis=-1, keepdims=True))
    return centered * lax.rsqrt(variance + EPS) * (1.0 + scale_by) + shift_by

def forward(tokens, cond_vec, ada_weight, qkv_weight, proj_weight, up_weight, down_weight, ada_bias, qv_bias, proj_bias, up_bias, down_bias):
    modulation = low_back(jnp.dot(low(jax.nn.silu(cond_vec)), ada_weight, precision=PRECISE) + ada_bias)
    pieces = modulation.reshape(6, D)
    normed = low(modulate(tokens, pieces[0], pieces[1]))
    full_bias = jnp.concatenate([qv_bias[:D], jnp.zeros((D,), jnp.float32), qv_bias[D:]])
    projected = low_back(low(jnp.dot(normed, qkv_weight, precision=PRECISE) + full_bias))
    projected = projected.reshape(LENGTH, 3, H, HD)
    queries = projected[:, 0]
    key_rows = projected[:, 1]
    value_rows = projected[:, 2]
    scores = low_back(jnp.einsum('qhd,khd->hqk', queries, key_rows, precision=PRECISE) * HD ** (-0.5))
    probs = low(jax.nn.softmax(scores, axis=-1))
    mixed = low_back(low(jnp.einsum('hqk,khd->qhd', probs, value_rows, precision=PRECISE)))
    mixed = mixed.reshape(LENGTH, D)
    attn_out = low_back(jnp.dot(mixed, proj_weight, precision=PRECISE) + proj_bias)
    middle = tokens + pieces[2] * attn_out
    normed_two = low(modulate(middle, pieces[3], pieces[4]))
    pre_act = low_back(jnp.dot(normed_two, up_weight, precision=PRECISE) + up_bias)
    hidden = low(jax.nn.gelu(pre_act, approximate=True))
    mlp_out = low_back(jnp.dot(hidden, down_weight, precision=PRECISE) + down_bias)
    return middle + pieces[5] * mlp_out

def reference(hidden_in, condition, out_grad, ada_weight, qkv_weight, proj_weight, up_weight, down_weight, ada_bias, qv_bias, proj_bias, up_bias, down_bias):
    params = tuple((weight_arg.astype(jnp.float32) for weight_arg in (ada_weight, qkv_weight, proj_weight, up_weight, down_weight, ada_bias, qv_bias, proj_bias, up_bias, down_bias)))

    def per_latent(totals, latent):
        tokens, cond_vec, cotangent = latent
        result, backward = jax.vjp(forward, tokens.astype(jnp.float32), cond_vec.astype(jnp.float32), *params)
        grads = backward(cotangent.astype(jnp.float32))
        totals = tuple((total_part + grad_part for total_part, grad_part in zip(totals, grads[2:])))
        return (totals, (result.astype(jnp.bfloat16), grads[0], grads[1]))
    start = tuple((jnp.zeros_like(param) for param in params))
    totals, stacked = lax.scan(per_latent, start, (hidden_in, condition, out_grad))
    return (stacked[0], stacked[1], stacked[2], totals[0], totals[1], totals[2], totals[3], totals[4], totals[5], totals[6], totals[7], totals[8], totals[9])
```

```python
from functools import partial

import jax
import jax.numpy as jnp
from jax import lax
from jax.sharding import PartitionSpec as P

HD = 64


EPS = 1e-06

AXES = ("shard", "seq")

bf16 = jnp.bfloat16
f32 = jnp.float32


def modulate(tokens, shift_by, scale_by):
    average = jnp.mean(tokens, axis=-1, keepdims=True)
    centered = tokens - average
    variance = jnp.mean(centered * centered, axis=-1, keepdims=True)
    return centered * lax.rsqrt(variance + EPS) * (1.0 + scale_by) + shift_by


def cross_rows(left, right):
    return lax.dot_general(left, right, (((0,), (0,)), ((), ())), preferred_element_type=f32)


def along_cols(left, right):
    return lax.dot_general(left, right, (((1,), (1,)), ((), ())), preferred_element_type=f32)


def plain(left, right):
    return jnp.dot(left, right, preferred_element_type=f32)


def attend_forward(queries, key_rows, value_rows):
    factor = HD ** (-0.5)
    count = queries.shape[0]
    queries = queries.reshape(count, -1, HD)
    key_rows = key_rows.reshape(key_rows.shape[0], -1, HD)
    value_rows = value_rows.reshape(value_rows.shape[0], -1, HD)
    scores = factor * jnp.einsum("qhd,khd->hqk", queries, key_rows, preferred_element_type=f32)
    highest = jnp.max(scores, axis=-1, keepdims=True)
    expon = jnp.exp(scores - highest)
    summed = jnp.sum(expon, axis=-1, keepdims=True)
    probs = (expon / summed).astype(bf16)
    mixed = jnp.einsum("hqk,khd->qhd", probs, value_rows, preferred_element_type=f32)
    return mixed.astype(bf16).reshape(count, -1), (highest + jnp.log(summed))[..., 0]


def attend_backward(queries, key_rows, value_rows, log_sums, grad_mixed):
    factor = HD ** (-0.5)
    count = queries.shape[0]
    length = key_rows.shape[0]
    queries = queries.reshape(count, -1, HD)
    grad_rows = grad_mixed.reshape(count, -1, HD)
    key_rows = key_rows.reshape(length, -1, HD)
    value_rows = value_rows.reshape(length, -1, HD)
    scores = factor * jnp.einsum("qhd,khd->hqk", queries, key_rows, preferred_element_type=f32)
    probs = jnp.exp(scores - log_sums[..., None])
    grad_probs = jnp.einsum("qhd,khd->hqk", grad_rows, value_rows, preferred_element_type=f32)
    inner = jnp.sum(probs * grad_probs, axis=-1, keepdims=True)
    grad_scores = (probs * (grad_probs - inner)).astype(bf16)
    grad_values = jnp.einsum("hqk,qhd->khd", probs.astype(bf16), grad_rows, preferred_element_type=f32)
    grad_queries = factor * jnp.einsum("hqk,khd->qhd", grad_scores, key_rows, preferred_element_type=f32)
    grad_keys = factor * jnp.einsum("hqk,qhd->khd", grad_scores, queries, preferred_element_type=f32)
    return (
        grad_queries.reshape(count, -1),
        grad_keys.reshape(length, -1),
        grad_values.reshape(length, -1),
    )


class Places:
    def __init__(self, latents):
        self.shards = lax.axis_size("shard")
        self.groups = lax.axis_size("seq")
        self.devices = self.shards * self.groups
        self.latents = latents
        assert 2 * latents == self.groups
        self.shard = lax.axis_index("shard")
        self.seq = lax.axis_index("seq")
        self.flat = self.shard * self.groups + self.seq
        self.core = self.shard % 2
        self.slot = self.seq % latents
        self.moves = []
        for turn in range(latents):
            move = []
            for source in range(self.devices):
                pair, core = divmod(source // self.groups, 2)
                half, place = divmod(source % self.groups, latents)
                member = (place + turn) % latents
                target = (2 * pair + half) * self.groups + core * latents + member
                move.append((source, target))
            self.moves.append(move)

    def to_pairs(self, blocks):
        parts = []
        for turn, move in enumerate(self.moves):
            member = (self.slot + turn) % self.latents
            block = lax.dynamic_index_in_dim(blocks, member, 0, keepdims=False)
            parts.append(lax.ppermute(block, AXES, move))
        return jnp.concatenate(parts, axis=0)

    def from_pairs(self, rows):
        tokens = rows.shape[0] // self.latents
        parts = []
        for turn, move in enumerate(self.moves):
            block = rows[turn * tokens : (turn + 1) * tokens]
            parts.append(lax.ppermute(block, AXES, [(b, a) for a, b in move]))
        twice = jnp.stack(parts + parts)
        start = (self.latents - self.slot) % self.latents
        return lax.dynamic_slice_in_dim(twice, start, self.latents, axis=0)

    def across(self, array, bit):
        swaps = [(s, s ^ (1 << bit)) for s in range(self.shards)]
        return lax.ppermute(array, "shard", swaps)

    def order(self, bits):
        order = [0]
        for bit in reversed(bits):
            order = order + [near ^ (1 << bit) for near in order]
        return order

    def arranged(self, matrix, bits):
        width = matrix.shape[1] // self.shards
        return jnp.concatenate(
            [
                lax.dynamic_slice_in_dim(matrix, (self.shard ^ near) * width, width, axis=1)
                for near in self.order(bits)
            ],
            axis=1,
        )

    def reduced(self, left, right, bits):
        columns = self.arranged(left, bits)
        width = columns.shape[1] // self.shards
        received = []

        def piece(low, high):
            total = cross_rows(columns[:, low * width : high * width], right)
            for part in received:
                total = total + part[low * width : high * width].astype(f32)
            return total

        for step, bit in enumerate(bits):
            low, high = self.shards >> (step + 1), self.shards >> step
            received.append(self.across(piece(low, high).astype(bf16), bit))
        own = piece(0, 1)
        rows = width // self.groups

        def block(away):
            begin = ((self.seq + away) % self.groups) * rows
            return lax.dynamic_slice_in_dim(own, begin, rows, axis=0)

        total = block(0)
        for away in range(1, self.groups):
            shift = [(q, (q + away) % self.groups) for q in range(self.groups)]
            total = total + lax.ppermute(block(away).astype(bf16), "seq", shift).astype(f32)
        return total


def shards(
    hidden_in,
    condition,
    out_grad,
    ada_weight,
    qkv_weight,
    proj_weight,
    up_weight,
    down_weight,
    ada_bias,
    qv_bias,
    proj_bias,
    up_bias,
    down_bias,
):
    latents, local_len, width = hidden_in.shape
    at = Places(latents)
    bits = list(range(at.shards.bit_length() - 1))
    bits_back = bits[:1] + bits[:0:-1]
    pairs = at.shards // 2
    total_latents = pairs * at.groups
    depth = ada_weight.shape[0]

    w_qkv = lax.all_gather(qkv_weight, AXES, axis=0, tiled=True)
    w_proj = lax.all_gather(proj_weight, AXES, axis=0, tiled=True)
    w_up = lax.all_gather(up_weight, AXES, axis=0, tiled=True)
    w_down = lax.all_gather(down_weight, AXES, axis=0, tiled=True)

    tokens = at.to_pairs(hidden_in).astype(f32)
    cotangent = at.to_pairs(out_grad).astype(f32)

    every_condition = lax.all_gather(condition, "shard", axis=0, tiled=True).astype(f32)
    silu_rows = lax.dynamic_slice_in_dim(every_condition, at.flat * depth, depth, axis=1)
    silu_rows = jax.nn.silu(silu_rows).astype(bf16)
    share = plain(silu_rows, ada_weight)
    wide = share.shape[1]
    share = share.reshape(pairs, at.groups, 2, wide // 2).transpose(0, 2, 1, 3)
    share = share.reshape(at.devices, wide // 2)
    biases = jnp.concatenate([ada_bias, qv_bias, proj_bias, up_bias, down_bias]).astype(f32)
    cuts = [ada_bias.shape[0], qv_bias.shape[0], proj_bias.shape[0], up_bias.shape[0], down_bias.shape[0]]
    sent = jnp.concatenate([share, jnp.broadcast_to(biases, (at.devices, biases.shape[0]))], axis=1)
    came = lax.all_to_all(sent, AXES, 0, 0, tiled=True)
    mine = jnp.sum(came[:, : wide // 2], axis=0)
    other = at.across(mine, 0)
    modulation = jnp.where(
        at.core == 0, jnp.concatenate([mine, other]), jnp.concatenate([other, mine])
    )
    whole = []
    begin = wide // 2
    for cut in cuts:
        whole.append(came[:, begin : begin + cut].reshape(-1))
        begin += cut
    b_ada, b_qv, b_proj, b_up, b_down = whole
    modulation = (modulation + b_ada).reshape(6, width)
    shift_a, scale_a, gate_a, shift_m, scale_m, gate_m = [modulation[member] for member in range(6)]

    normed = modulate(tokens, shift_a, scale_a).astype(bf16)
    kv_bias = jnp.concatenate([jnp.zeros((width,), f32), b_qv[width:]])
    kv_own = (plain(normed, w_qkv[:, width:]) + kv_bias).astype(bf16)
    kv_other = at.across(kv_own, 0)
    queries = (plain(normed, w_qkv[:, :width]) + b_qv[:width]).astype(bf16)
    kv_all = jnp.concatenate([kv_own, kv_other], axis=0)
    key_rows, value_rows = kv_all[:, :width], kv_all[:, width:]
    mixed, log_sums = attend_forward(queries, key_rows, value_rows)
    attn_out = plain(mixed, w_proj) + b_proj
    middle = tokens + gate_a * attn_out
    normed_two = modulate(middle, shift_m, scale_m).astype(bf16)
    pre_act = plain(normed_two, w_up) + b_up
    hidden = jax.nn.gelu(pre_act, approximate=True).astype(bf16)
    mlp_out = plain(hidden, w_down) + b_down
    block_out = at.from_pairs((middle + gate_m * mlp_out).astype(bf16))

    grad_gate_m = jnp.sum(cotangent * mlp_out, axis=0)
    grad_mlp = (gate_m * cotangent).astype(bf16)
    grad_bdown = jnp.sum(grad_mlp.astype(f32), axis=0)
    grad_hidden = along_cols(grad_mlp, w_down)
    _, gelu_back = jax.vjp(partial(jax.nn.gelu, approximate=True), pre_act)
    grad_pre = gelu_back(grad_hidden)[0].astype(bf16)
    grad_bup = jnp.sum(grad_pre.astype(f32), axis=0)
    down_share = at.reduced(hidden, grad_mlp, bits_back)
    up_share = at.reduced(normed_two, grad_pre, bits)
    grad_normed_two = along_cols(grad_pre, w_up)
    _, second_back = jax.vjp(modulate, middle, shift_m, scale_m)
    grad_middle, grad_shift_m, grad_scale_m = second_back(grad_normed_two)
    grad_middle = grad_middle + cotangent

    grad_gate_a = jnp.sum(grad_middle * attn_out, axis=0)
    grad_attn = (gate_a * grad_middle).astype(bf16)
    grad_bproj = jnp.sum(grad_attn.astype(f32), axis=0)
    grad_mixed = along_cols(grad_attn, w_proj).astype(bf16)
    proj_share = at.reduced(mixed, grad_attn, bits)
    grad_queries, grad_keys, grad_values = attend_backward(
        queries, key_rows, value_rows, log_sums, grad_mixed
    )
    count = tokens.shape[0]
    grad_kv = jnp.concatenate([grad_keys, grad_values], axis=1)
    kv_came = at.across(grad_kv[count:].astype(bf16), 0)
    grad_kv = (grad_kv[:count] + kv_came.astype(f32)).astype(bf16)
    grad_rows = jnp.concatenate([grad_queries.astype(bf16), grad_kv], axis=1)
    qkv_share = at.reduced(normed, grad_rows, bits)
    column_sums = jnp.sum(grad_rows.astype(f32), axis=0)
    grad_bqv = jnp.concatenate([column_sums[:width], column_sums[2 * width :]])
    grad_normed = along_cols(grad_rows, w_qkv)
    _, first_back = jax.vjp(modulate, tokens, shift_a, scale_a)
    grad_tokens, grad_shift_a, grad_scale_a = first_back(grad_normed)
    hidden_grad = at.from_pairs((grad_tokens + grad_middle).astype(bf16)).astype(f32)

    part_mod = jnp.concatenate(
        [grad_shift_a, grad_scale_a, grad_gate_a, grad_shift_m, grad_scale_m, grad_gate_m]
    )
    grad_mod = (part_mod + at.across(part_mod, 0)).astype(bf16)
    half_mod = lax.dynamic_slice_in_dim(grad_mod, at.core * (wide // 2), wide // 2).astype(f32)
    bias_parts = [
        part.reshape(at.devices, -1) for part in (grad_bqv, grad_bproj, grad_bup, grad_bdown)
    ]
    sent = jnp.concatenate(
        [jnp.broadcast_to(half_mod, (at.devices, wide // 2))] + bias_parts, axis=1
    )
    came = lax.all_to_all(sent, AXES, 0, 0, tiled=True)
    every_mod = came[:, : wide // 2].reshape(pairs, 2, at.groups, wide // 2)
    every_mod = every_mod.transpose(0, 2, 1, 3).reshape(total_latents, wide).astype(bf16)
    bias_sums = jnp.sum(came[:, wide // 2 :], axis=0)
    bias_shares = []
    begin = 0
    for part in bias_parts:
        bias_shares.append(bias_sums[begin : begin + part.shape[1]])
        begin += part.shape[1]
    ada_share = cross_rows(silu_rows, every_mod)
    own_bias = ada_bias.shape[0]
    adabias_share = jnp.sum(
        lax.dynamic_slice_in_dim(every_mod, at.flat * own_bias, own_bias, axis=1).astype(f32), axis=0
    )
    grad_silu = along_cols(every_mod, ada_weight).reshape(at.shards, 1, latents * depth)
    sent = jnp.broadcast_to(grad_silu, (at.shards, at.groups, latents * depth))
    came = lax.all_to_all(sent.reshape(at.devices, latents * depth), AXES, 0, 0, tiled=True)
    grad_silu = came.reshape(at.devices, latents, depth).transpose(1, 0, 2).reshape(latents, width)
    _, silu_back = jax.vjp(jax.nn.silu, condition.astype(f32))
    condition_grad = silu_back(grad_silu)[0]
    return (
        block_out,
        hidden_grad,
        condition_grad,
        ada_share,
        qkv_share,
        proj_share,
        up_share,
        down_share,
        adabias_share,
        bias_shares[0],
        bias_shares[1],
        bias_shares[2],
        bias_shares[3],
    )


def solution(mesh):
    in_specs = (
        P("shard", "seq", None),
        P("shard", None),
        P("shard", "seq", None),
        P(("shard", "seq"), None),
        P(("shard", "seq"), None),
        P(("shard", "seq"), None),
        P(("shard", "seq"), None),
        P(("shard", "seq"), None),
        P(("shard", "seq")),
        P(("shard", "seq")),
        P(("shard", "seq")),
        P(("shard", "seq")),
        P(("shard", "seq")),
    )
    out_specs = (
        P("shard", "seq", None),
        P("shard", "seq", None),
        P("shard", None),
        P(("shard", "seq"), None),
        P(("shard", "seq"), None),
        P(("shard", "seq"), None),
        P(("shard", "seq"), None),
        P(("shard", "seq"), None),
        P(("shard", "seq")),
        P(("shard", "seq")),
        P(("shard", "seq")),
        P(("shard", "seq")),
        P(("shard", "seq")),
    )
    return jax.shard_map(shards, mesh=mesh, in_specs=in_specs, out_specs=out_specs, check_vma=False)
```

```python
from functools import partial

import jax
import jax.numpy as jnp
from jax import lax
from jax.experimental import pallas as pl
from jax.experimental.pallas import tpu as pltpu
from jax.sharding import PartitionSpec as P

HD = 64


EPS = 1e-06

AXES = ("shard", "seq")

bf16 = jnp.bfloat16
f32 = jnp.float32


def modulate(tokens, shift_by, scale_by):
    average = jnp.mean(tokens, axis=-1, keepdims=True)
    centered = tokens - average
    variance = jnp.mean(centered * centered, axis=-1, keepdims=True)
    return centered * lax.rsqrt(variance + EPS) * (1.0 + scale_by) + shift_by


def cross_rows(left, right):
    return lax.dot_general(left, right, (((0,), (0,)), ((), ())), preferred_element_type=f32)


def along_cols(left, right):
    return lax.dot_general(left, right, (((1,), (1,)), ((), ())), preferred_element_type=f32)


def plain(left, right):
    return jnp.dot(left, right, preferred_element_type=f32)


LIMIT = 48 * 1024 * 1024


def call(kernel, flops, **kwargs):
    return pl.pallas_call(
        kernel,
        compiler_params=pltpu.CompilerParams(vmem_limit_bytes=LIMIT),
        cost_estimate=pl.CostEstimate(flops=flops // 50, bytes_accessed=flops // 10000, transcendentals=0),
        **kwargs,
    )


def transposed_dot(left, right):
    return lax.dot_general(left, right, (((1,), (1,)), ((), ())), preferred_element_type=f32)


def project_kernel(x_ref, low_ref, high_ref, bias_ref, out_ref):
    half = low_ref.shape[0]
    total = jnp.dot(x_ref[:, :half], low_ref[...], preferred_element_type=f32)
    total = total + jnp.dot(x_ref[:, half:], high_ref[...], preferred_element_type=f32)
    out_ref[...] = (total + bias_ref[...]).astype(out_ref.dtype)


def project(x, weight, begin, columns, bias, dtype):
    low, high = weight
    rows, depth = x.shape
    tile = 512
    first = begin // tile
    pick = lambda step: (0, first + step)
    return call(
        project_kernel,
        2 * rows * depth * columns,
        grid=(columns // tile,),
        in_specs=[
            pl.BlockSpec((rows, depth), lambda step: (0, 0)),
            pl.BlockSpec((depth // 2, tile), pick),
            pl.BlockSpec((depth // 2, tile), pick),
            pl.BlockSpec((1, tile), lambda step: (0, step)),
        ],
        out_specs=pl.BlockSpec((rows, tile), lambda step: (0, step)),
        out_shape=jax.ShapeDtypeStruct((rows, columns), dtype),
    )(x, low, high, bias.reshape(1, -1))


def unproject_kernel(rows_ref, weight_ref, out_ref):
    width = rows_ref.shape[2]
    total = transposed_dot(rows_ref[0], weight_ref[:, :width])
    total = total + transposed_dot(rows_ref[1], weight_ref[:, width : 2 * width])
    out_ref[...] = total + transposed_dot(rows_ref[2], weight_ref[:, 2 * width :])


def unproject(rows, weight):
    _, count, width = rows.shape
    depth = weight.shape[0]
    tile = 256
    return call(
        unproject_kernel,
        6 * count * depth * width,
        grid=(depth // tile,),
        in_specs=[
            pl.BlockSpec((3, count, width), lambda step: (0, 0, 0)),
            pl.BlockSpec((tile, 3 * width), lambda step: (step, 0)),
        ],
        out_specs=pl.BlockSpec((count, tile), lambda step: (0, step)),
        out_shape=jax.ShapeDtypeStruct((count, depth), f32),
    )(rows, weight)


def attend_forward_kernel(q_ref, *refs):
    keys, values = refs[0:2], refs[2:4]
    out_ref, log_ref = refs[4:]
    count = q_ref.shape[0]
    outputs = []
    for head in range(2):
        cols = slice(head * HD, (head + 1) * HD)
        query = q_ref[:, cols] * jnp.bfloat16(HD ** (-0.5))
        scores = [transposed_dot(query, key[:, cols]) for key in keys]
        highest = jnp.maximum(
            jnp.max(scores[0], axis=1, keepdims=True), jnp.max(scores[1], axis=1, keepdims=True)
        )
        expon = [jnp.exp(score - highest) for score in scores]
        summed = jnp.sum(expon[0], axis=1, keepdims=True) + jnp.sum(expon[1], axis=1, keepdims=True)
        mixed = jnp.dot(expon[0].astype(bf16), values[0][:, cols], preferred_element_type=f32)
        mixed = mixed + jnp.dot(expon[1].astype(bf16), values[1][:, cols], preferred_element_type=f32)
        outputs.append(mixed / summed)
        logs = jnp.broadcast_to(highest + jnp.log(summed), (count, 128))
        log_ref[head] = jnp.transpose(logs)[0:1]
    out_ref[...] = jnp.concatenate(outputs, axis=1).astype(bf16)


def attend_forward(queries, keys, values):
    count, width = queries.shape
    pair = pl.BlockSpec((count, 2 * HD), lambda step: (0, step))
    steps = width // (2 * HD)
    return call(
        attend_forward_kernel,
        16 * count * count * width,
        grid=(steps,),
        in_specs=[pair] * 5,
        out_specs=[pair, pl.BlockSpec((2, 1, count), lambda step: (step, 0, 0))],
        out_shape=[
            jax.ShapeDtypeStruct((count, width), bf16),
            jax.ShapeDtypeStruct((2 * steps, 1, count), f32),
        ],
    )(queries, *keys, *values)


def attend_backward_kernel(q_ref, g_ref, log_ref, *refs):
    keys, values = refs[0:2], refs[2:4]
    own_ref, other_ref = refs[-2:]
    grads = [[], [], [], [], []]
    factor = HD ** (-0.5)
    for head in range(2):
        cols = slice(head * HD, (head + 1) * HD)
        query = q_ref[:, cols] * jnp.bfloat16(factor)
        grad = g_ref[:, cols]
        logs = log_ref[head]
        probs = [jnp.exp(transposed_dot(key[:, cols], query) - logs) for key in keys]
        grad_probs = [transposed_dot(value[:, cols], grad) for value in values]
        inner = jnp.sum(probs[0] * grad_probs[0], axis=0, keepdims=True)
        inner = inner + jnp.sum(probs[1] * grad_probs[1], axis=0, keepdims=True)
        grad_query = 0.0
        for side in range(2):
            grad_scores = (probs[side] * (grad_probs[side] - inner)).astype(bf16)
            grads[1 + 2 * side].append(jnp.dot(grad_scores, query, preferred_element_type=f32))
            grads[2 + 2 * side].append(
                jnp.dot(probs[side].astype(bf16), grad, preferred_element_type=f32)
            )
            grad_query = grad_query + cross_rows(grad_scores, keys[side][:, cols])
        grads[0].append(factor * grad_query)
    joined = [jnp.concatenate(part, axis=1).astype(bf16) for part in grads]
    for place in range(3):
        own_ref[place] = joined[place]
    for place in range(2):
        other_ref[place] = joined[3 + place]


def attend_backward(queries, grad_mixed, logs, keys, values, begin, steps, so_far):
    count, width = queries.shape
    pair = pl.BlockSpec((count, 2 * HD), lambda step: (0, begin + step))
    own = pl.BlockSpec((3, count, 2 * HD), lambda step: (0, 0, begin + step))
    other = pl.BlockSpec((2, count, 2 * HD), lambda step: (0, 0, begin + step))
    log_spec = pl.BlockSpec((2, 1, count), lambda step: (begin + step, 0, 0))
    operands = [queries, grad_mixed, logs, *keys, *values]
    specs = [pair, pair, log_spec] + [pair] * 4
    aliases = {}
    if so_far is not None:
        aliases = {len(operands): 0, len(operands) + 1: 1}
        operands = operands + list(so_far)
        specs = specs + [pl.BlockSpec(memory_space=pl.ANY)] * 2
    return call(
        attend_backward_kernel,
        40 * count * count * 2 * HD * steps,
        grid=(steps,),
        in_specs=specs,
        out_specs=[own, other],
        out_shape=[
            jax.ShapeDtypeStruct((3, count, width), bf16),
            jax.ShapeDtypeStruct((2, count, width), bf16),
        ],
        input_output_aliases=aliases,
    )(*operands)


def mlp_forward_kernel(x_ref, up_ref, down_ref, up_bias_ref, down_bias_ref, hidden_ref, slope_ref, out_ref):
    tile = hidden_ref.shape[1]
    pre = jnp.dot(x_ref[...], up_ref[...].reshape(-1, tile), preferred_element_type=f32)
    pre = pre + up_bias_ref[...]
    root, cubic = 0.7978845608028654, 0.044715
    square = pre * pre
    wave = jnp.tanh(root * pre * (1.0 + cubic * square))
    half = 0.5 * (1.0 + wave)
    slope = half + 0.5 * pre * (1.0 - wave * wave) * (root * (1.0 + 3.0 * cubic * square))
    slope_ref[...] = slope.astype(bf16)
    hidden = (pre * half).astype(bf16)
    hidden_ref[...] = hidden
    down = down_ref[...].reshape(tile, -1)

    @pl.when(pl.program_id(0) == 0)
    def _():
        out_ref[...] = jnp.broadcast_to(down_bias_ref[...], out_ref.shape)

    out_ref[...] += jnp.dot(hidden, down, preferred_element_type=f32)


def mlp_forward(x, mlp, up_bias, down_bias):
    count, width = x.shape
    hidden_width = up_bias.shape[0]
    tile = 512
    whole = pl.BlockSpec((count, width), lambda step: (0, 0))
    part = pl.BlockSpec((count, tile), lambda step: (0, step))
    return call(
        mlp_forward_kernel,
        4 * count * width * hidden_width,
        grid=(hidden_width // tile,),
        in_specs=[whole]
        + mlp.specs(tile)
        + [
            pl.BlockSpec((1, tile), lambda step: (0, step)),
            pl.BlockSpec((1, width), lambda step: (0, 0)),
        ],
        out_specs=[part, part, whole],
        out_shape=[
            jax.ShapeDtypeStruct((count, hidden_width), bf16),
            jax.ShapeDtypeStruct((count, hidden_width), bf16),
            jax.ShapeDtypeStruct((count, width), f32),
        ],
    )(x, *mlp.arrays, up_bias.reshape(1, -1), down_bias.reshape(1, -1))


def mlp_backward_kernel(grad_ref, up_ref, down_ref, slope_ref, grad_pre_ref, sums_ref, out_ref):
    tile = slope_ref.shape[1]
    grad_hidden = transposed_dot(grad_ref[...], down_ref[...].reshape(tile, -1))
    grad_pre = (grad_hidden * slope_ref[...].astype(f32)).astype(bf16)
    grad_pre_ref[...] = grad_pre
    sums_ref[...] = jnp.sum(grad_pre.astype(f32), axis=0, keepdims=True)

    @pl.when(pl.program_id(0) == 0)
    def _():
        out_ref[...] = jnp.zeros(out_ref.shape, f32)

    out_ref[...] += transposed_dot(grad_pre, up_ref[...].reshape(-1, tile))


def mlp_backward(grad, mlp, slope):
    count, width = grad.shape
    hidden_width = slope.shape[1]
    tile = 512
    whole = pl.BlockSpec((count, width), lambda step: (0, 0))
    part = pl.BlockSpec((count, tile), lambda step: (0, step))
    return call(
        mlp_backward_kernel,
        4 * count * width * hidden_width,
        grid=(hidden_width // tile,),
        in_specs=[whole] + mlp.specs(tile) + [part],
        out_specs=[part, pl.BlockSpec((1, tile), lambda step: (0, step)), whole],
        out_shape=[
            jax.ShapeDtypeStruct((count, hidden_width), bf16),
            jax.ShapeDtypeStruct((1, hidden_width), f32),
            jax.ShapeDtypeStruct((count, width), f32),
        ],
    )(grad, *mlp.arrays, slope)


class FeedForward:
    def __init__(self, up, down):
        self.rows_up, hidden_width = up.shape
        self.rows_down, self.width = down.shape
        cut_up = up.reshape(self.rows_up, -1, self.width).transpose(1, 0, 2).reshape(-1, self.width)
        both = lax.all_gather(jnp.concatenate([cut_up, down], axis=0), AXES, axis=0, tiled=False)
        self.in_place = self.rows_up % 16 == 0 and self.rows_down == cut_up.shape[0]
        if self.in_place:
            self.arrays = (both, both)
        else:
            devices = both.shape[0]
            up = both[:, : cut_up.shape[0]].reshape(devices, -1, self.rows_up, self.width)
            up = up.transpose(0, 2, 1, 3).reshape(1, devices * self.rows_up, hidden_width)
            down = both[:, cut_up.shape[0] :].reshape(1, hidden_width, self.width)
            self.arrays = (up, down)

    def specs(self, tile):
        up, down = self.arrays
        if not self.in_place:
            return [
                pl.BlockSpec((1, up.shape[1], tile), lambda step: (0, 0, step)),
                pl.BlockSpec((1, tile, self.width), lambda step: (0, step, 0)),
            ]
        across = self.width // tile
        return [
            pl.BlockSpec(
                (up.shape[0], self.rows_up, tile), lambda step: (0, step // across, step % across)
            ),
            pl.BlockSpec(
                (tile // self.rows_down, self.rows_down, self.width), lambda step: (step, 1, 0)
            ),
        ]


class Places:
    def __init__(self, latents):
        self.shards = lax.axis_size("shard")
        self.groups = lax.axis_size("seq")
        self.devices = self.shards * self.groups
        self.latents = latents
        assert 2 * latents == self.groups
        self.shard = lax.axis_index("shard")
        self.seq = lax.axis_index("seq")
        self.flat = self.shard * self.groups + self.seq
        self.core = self.shard % 2
        self.slot = self.seq % latents
        self.moves = []
        for turn in range(latents):
            move = []
            for source in range(self.devices):
                pair, core = divmod(source // self.groups, 2)
                half, place = divmod(source % self.groups, latents)
                member = (place + turn) % latents
                target = (2 * pair + half) * self.groups + core * latents + member
                move.append((source, target))
            self.moves.append(move)

    def to_pairs(self, blocks):
        parts = []
        for turn, move in enumerate(self.moves):
            member = (self.slot + turn) % self.latents
            block = lax.dynamic_index_in_dim(blocks, member, 0, keepdims=False)
            parts.append(lax.ppermute(block, AXES, move))
        return parts

    def from_pairs(self, rows):
        tokens = rows.shape[0] // self.latents
        parts = []
        for turn, move in enumerate(self.moves):
            block = rows[turn * tokens : (turn + 1) * tokens]
            parts.append(lax.ppermute(block, AXES, [(b, a) for a, b in move]))
        return parts

    def placed(self, parts):
        if len(parts) == 2:
            straight = self.slot == 0
            return jnp.stack(
                [jnp.where(straight, parts[0], parts[1]), jnp.where(straight, parts[1], parts[0])]
            )
        twice = jnp.stack(parts + parts)
        start = (self.latents - self.slot) % self.latents
        return lax.dynamic_slice_in_dim(twice, start, self.latents, axis=0)

    def across(self, array, mask=1):
        return lax.ppermute(array, "shard", [(s, s ^ mask) for s in range(self.shards)])

    def order(self):
        near = list(range(0, self.shards, 2))
        return near + [each ^ 1 for each in near]

    def arranged(self, matrix):
        width = matrix.shape[1] // self.shards
        return jnp.concatenate(
            [
                lax.dynamic_slice_in_dim(matrix, (self.shard ^ near) * width, width, axis=1)
                for near in self.order()
            ],
            axis=1,
        )

    def restored(self, matrix):
        width = matrix.shape[1] // self.shards
        order = self.order()
        places = jnp.array([order.index(near) for near in range(self.shards)], jnp.int32)
        return jnp.concatenate(
            [
                lax.dynamic_slice_in_dim(matrix, places[self.shard ^ s] * width, width, axis=1)
                for s in range(self.shards)
            ],
            axis=1,
        )

    def along_seq(self, block):
        parts = [block]
        for away in range(self.groups - 1, 0, -1):
            shift = [(q, (q + away) % self.groups) for q in range(self.groups)]
            parts.append(lax.ppermute(block, "seq", shift))
        start = ((self.groups - self.seq) % self.groups) * block.shape[0]
        twice = jnp.concatenate(parts + parts, axis=0)
        return lax.dynamic_slice_in_dim(twice, start, block.shape[0] * self.groups, axis=0)

    def gathered(self, block):
        parts = [block] + [self.across(block, mask) for mask in range(2, self.shards, 2)]
        return parts


class Reduction:
    def __init__(self, at, columns, right):
        self.at, self.columns, self.right = at, columns, right
        self.width = columns.shape[1] // at.shards
        self.received = []

    def piece(self, low, high):
        low, high = low * self.width, high * self.width
        left = self.columns[:, low:high]
        if self.right.ndim == 3:
            total = jnp.einsum("tm,ptn->pmn", left, self.right, preferred_element_type=f32)
        else:
            total = cross_rows(left, self.right)
        if self.received:
            total = total + self.received[0][..., low:high, :].astype(f32)
        return total

    def first(self):
        half = self.at.shards // 2
        return self.piece(half, 2 * half).astype(bf16)

    def send_first(self, block):
        self.received = [self.at.across(block)]

    def middle(self):
        return [self.piece(each, each + 1).astype(bf16) for each in range(1, self.at.shards // 2)]

    def send_middle(self, blocks):
        for each, block in enumerate(blocks):
            self.received.append(self.at.across(block, 2 * (each + 1)))

    def last(self):
        total = self.piece(0, 1)
        for part in self.received[1:]:
            total = total + part.astype(f32)
        return total.astype(bf16)

    def swap_last(self, block):
        groups = self.at.groups
        came = lax.all_to_all(block, "seq", 0, 0, tiled=True)
        return list(came.reshape(groups, -1, block.shape[1]))

    def split_last(self, total):
        at = self.at
        rows = self.width // at.groups

        def block(away):
            begin = ((at.seq + away) % at.groups) * rows
            return lax.dynamic_slice_in_dim(total, begin, rows, axis=total.ndim - 2)

        return [block(away) for away in range(at.groups)]

    def send_last(self, blocks):
        at = self.at
        came = []
        for away in range(1, at.groups):
            shift = [(q, (q + away) % at.groups) for q in range(at.groups)]
            came.append(lax.ppermute(blocks[away], "seq", shift))
        return blocks[:1] + came


def total_of(blocks):
    total = blocks[0].astype(f32)
    for block in blocks[1:]:
        total = total + block.astype(f32)
    return total


def tied(*arrays):
    return lax.optimization_barrier(arrays)


def shards(
    hidden_in,
    condition,
    out_grad,
    ada_weight,
    qkv_weight,
    proj_weight,
    up_weight,
    down_weight,
    ada_bias,
    qv_bias,
    proj_bias,
    up_bias,
    down_bias,
):
    latents, local_len, width = hidden_in.shape
    at = Places(latents)
    pairs = at.shards // 2
    total_latents = pairs * at.groups
    depth = ada_weight.shape[0]

    mlp = FeedForward(up_weight, down_weight)
    near_rows = at.along_seq(jnp.concatenate([qkv_weight, proj_weight], axis=1))

    silu_rows = jax.nn.silu(condition.astype(f32)).astype(bf16)
    silu_rows = silu_rows.reshape(latents, at.shards, at.groups, depth)
    silu_rows = lax.dynamic_index_in_dim(silu_rows, at.seq, 2, keepdims=False)
    silu_rows = silu_rows.transpose(1, 0, 2).reshape(at.shards, latents * depth)
    silu_rows = lax.all_to_all(silu_rows, "shard", 0, 0, tiled=True).reshape(total_latents, depth)
    share = plain(silu_rows, ada_weight)
    wide = share.shape[1]
    share = share.reshape(pairs, at.groups, 2, wide // 2).transpose(0, 2, 1, 3)
    share = share.reshape(at.devices, wide // 2)
    biases = jnp.concatenate([ada_bias, qv_bias, proj_bias, up_bias, down_bias]).astype(f32)
    cuts = [ada_bias.shape[0], qv_bias.shape[0], proj_bias.shape[0], up_bias.shape[0], down_bias.shape[0]]
    sent = jnp.concatenate([share, jnp.broadcast_to(biases, (at.devices, biases.shape[0]))], axis=1)
    sent, near_rows, hidden_in = tied(sent, near_rows, hidden_in)
    came = lax.all_to_all(sent, AXES, 0, 0, tiled=True)
    near_parts = at.gathered(near_rows)
    tokens = at.to_pairs(hidden_in)
    came, *tokens = tied(came, *tokens)
    mine = jnp.sum(came[:, : wide // 2], axis=0)
    other = at.across(mine)
    modulation = jnp.where(
        at.core == 0, jnp.concatenate([mine, other]), jnp.concatenate([other, mine])
    )
    whole = []
    begin = wide // 2
    for cut in cuts:
        whole.append(came[:, begin : begin + cut].reshape(-1))
        begin += cut
    b_ada, b_qv, b_proj, b_up, b_down = whole
    modulation = (modulation + b_ada).reshape(6, width)
    shift_a, scale_a, gate_a, shift_m, scale_m, gate_m = [modulation[member] for member in range(6)]

    tokens = jnp.concatenate(tokens, axis=0).astype(f32)
    normed = modulate(tokens, shift_a, scale_a).astype(bf16)
    normed_cols = at.arranged(normed)
    normed_cols, *near_parts = tied(normed_cols, *near_parts)
    weight = jnp.concatenate(near_parts, axis=0)
    weight = (weight, at.across(weight))
    key_own = project(normed_cols, weight, width, width, jnp.zeros((width,), f32), bf16)
    keys = (key_own, at.across(key_own))
    value_own = project(normed_cols, weight, 2 * width, width, b_qv[width:], bf16)
    values = (value_own, at.across(value_own))
    queries = project(normed_cols, weight, 0, width, b_qv[:width], bf16)
    queries, out_grad = tied(queries, out_grad)
    cotangent = at.to_pairs(out_grad)
    mixed, logs = attend_forward(queries, keys, values)
    mixed_cols = at.arranged(mixed)
    attn_out = project(mixed_cols, weight, 3 * width, width, b_proj, f32)
    middle = tokens + gate_a * attn_out
    normed_two = modulate(middle, shift_m, scale_m).astype(bf16)
    hidden, slope, mlp_out = mlp_forward(normed_two, mlp, b_up, b_down)
    hidden, *cotangent = tied(hidden, *cotangent)
    block_rows = (middle + gate_m * mlp_out).astype(bf16)

    cotangent = jnp.concatenate(cotangent, axis=0).astype(f32)
    grad_gate_m = jnp.sum(cotangent * mlp_out, axis=0)
    grad_mlp = (gate_m * cotangent).astype(bf16)
    grad_bdown = jnp.sum(grad_mlp.astype(f32), axis=0)
    down_sum = Reduction(at, at.arranged(hidden), grad_mlp)
    slope, block, block_rows = tied(slope, down_sum.first(), block_rows)
    down_sum.send_first(block)
    block_out = at.from_pairs(block_rows)
    grad_pre, grad_bup, grad_normed_two = mlp_backward(grad_mlp, mlp, slope)
    grad_pre, grad_normed_two, *down_sum.received = tied(
        grad_pre, grad_normed_two, *down_sum.received
    )
    up_sum = Reduction(at, at.arranged(normed_two), grad_pre)
    grad_normed_two, block, *blocks = tied(grad_normed_two, up_sum.first(), *down_sum.middle())
    down_sum.send_middle(blocks)
    up_sum.send_first(block)
    _, second_back = jax.vjp(modulate, middle, shift_m, scale_m)
    grad_middle, grad_shift_m, grad_scale_m = second_back(grad_normed_two)
    grad_middle = grad_middle + cotangent

    grad_gate_a = jnp.sum(grad_middle * attn_out, axis=0)
    grad_attn = (gate_a * grad_middle).astype(bf16)
    grad_bproj = jnp.sum(grad_attn.astype(f32), axis=0)
    grad_mixed = jnp.concatenate(
        [along_cols(grad_attn, half[:, 3 * width :]).astype(bf16) for half in weight], axis=1
    )
    grad_mixed = at.restored(grad_mixed)
    proj_sum = Reduction(at, mixed_cols, grad_attn)
    grad_mixed, *up_sum.received = tied(grad_mixed, *up_sum.received)
    grad_mixed, block, *blocks = tied(grad_mixed, proj_sum.first(), *up_sum.middle())
    up_sum.send_middle(blocks)
    proj_sum.send_first(block)
    head_pairs = width // (2 * HD)
    cut = head_pairs // 2
    grads = attend_backward(queries, grad_mixed, logs, keys, values, 0, cut, None)
    *grads, proj_sum.received, down_sum.received, block_out = tied(
        *grads, proj_sum.received, down_sum.received, block_out
    )
    *grads, block = tied(*grads, down_sum.last())
    down_came = down_sum.swap_last(block)
    own_grads, other_grads = attend_backward(
        queries, grad_mixed, logs, keys, values, cut, head_pairs - cut, grads
    )
    own_grads, other_grads, down_came, up_sum.received = tied(
        own_grads, other_grads, down_came, up_sum.received
    )
    other_grads, up_block, *blocks = tied(other_grads, up_sum.last(), *proj_sum.middle())
    kv_came = at.across(other_grads)
    up_came = up_sum.swap_last(up_block)
    proj_sum.send_middle(blocks)
    grad_rows = jnp.concatenate([own_grads[:1], own_grads[1:] + kv_came], axis=0)
    qkv_sum = Reduction(at, normed_cols, grad_rows)
    grad_rows, block = tied(grad_rows, qkv_sum.first())
    qkv_sum.send_first(block)
    down_share = total_of(down_came)
    column_sums = jnp.sum(grad_rows.astype(f32), axis=1)
    grad_bqv = jnp.concatenate([column_sums[0], column_sums[2]])
    grad_normed = [unproject(grad_rows, weight[0])]
    grad_normed[0], qkv_sum.received, proj_sum.received = tied(
        grad_normed[0], qkv_sum.received, proj_sum.received
    )
    grad_rows, block, *blocks = tied(grad_rows, proj_sum.last(), *qkv_sum.middle())
    qkv_sum.send_middle(blocks)
    proj_came = proj_sum.swap_last(block)
    grad_normed.append(unproject(grad_rows, weight[1]))
    grad_normed = at.restored(jnp.concatenate(grad_normed, axis=1))
    _, first_back = jax.vjp(modulate, tokens, shift_a, scale_a)
    grad_tokens, grad_shift_a, grad_scale_a = first_back(grad_normed)
    hidden_rows = (grad_tokens + grad_middle).astype(bf16)

    part_mod = jnp.concatenate(
        [grad_shift_a, grad_scale_a, grad_gate_a, grad_shift_m, grad_scale_m, grad_gate_m]
    )
    part_mod, hidden_rows, up_came = tied(part_mod, hidden_rows, up_came)
    mod_came = at.across(part_mod)
    hidden_grad = at.from_pairs(hidden_rows)
    grad_mod = (part_mod + mod_came).astype(bf16)
    half_mod = lax.dynamic_slice_in_dim(grad_mod, at.core * (wide // 2), wide // 2).astype(f32)
    bias_parts = [
        part.reshape(at.devices, -1) for part in (grad_bqv, grad_bproj, grad_bup, grad_bdown)
    ]
    sent = jnp.concatenate(
        [jnp.broadcast_to(half_mod, (at.devices, wide // 2))] + bias_parts, axis=1
    )
    came = lax.all_to_all(sent, AXES, 0, 0, tiled=True)
    came, proj_came, hidden_grad, qkv_sum.received = tied(
        came, proj_came, hidden_grad, qkv_sum.received
    )
    came, block = tied(came, qkv_sum.last())
    qkv_came = qkv_sum.send_last(qkv_sum.split_last(block))
    up_share, proj_share = total_of(up_came), total_of(proj_came)
    every_mod = came[:, : wide // 2].reshape(pairs, 2, at.groups, wide // 2)
    every_mod = every_mod.transpose(0, 2, 1, 3).reshape(total_latents, wide).astype(bf16)
    bias_sums = jnp.sum(came[:, wide // 2 :], axis=0)
    bias_shares = []
    begin = 0
    for part in bias_parts:
        bias_shares.append(bias_sums[begin : begin + part.shape[1]])
        begin += part.shape[1]
    ada_share = cross_rows(silu_rows, every_mod)
    own_bias = ada_bias.shape[0]
    adabias_share = jnp.sum(
        lax.dynamic_slice_in_dim(every_mod, at.flat * own_bias, own_bias, axis=1).astype(f32), axis=0
    )
    grad_silu = along_cols(every_mod, ada_weight).reshape(at.shards, 1, latents * depth)
    sent = jnp.broadcast_to(grad_silu, (at.shards, at.groups, latents * depth))
    came = lax.all_to_all(sent.reshape(at.devices, latents * depth), AXES, 0, 0, tiled=True)
    grad_silu = came.reshape(at.devices, latents, depth).transpose(1, 0, 2).reshape(latents, width)
    _, silu_back = jax.vjp(jax.nn.silu, condition.astype(f32))
    condition_grad = silu_back(grad_silu)[0]
    qkv_share = total_of(qkv_came).transpose(1, 0, 2).reshape(-1, 3 * width)
    return (
        at.placed(block_out),
        at.placed(hidden_grad).astype(f32),
        condition_grad,
        ada_share,
        qkv_share,
        proj_share,
        up_share,
        down_share,
        adabias_share,
        bias_shares[0],
        bias_shares[1],
        bias_shares[2],
        bias_shares[3],
    )


def solution(mesh):
    in_specs = (
        P("shard", "seq", None),
        P("shard", None),
        P("shard", "seq", None),
        P(("shard", "seq"), None),
        P(("shard", "seq"), None),
        P(("shard", "seq"), None),
        P(("shard", "seq"), None),
        P(("shard", "seq"), None),
        P(("shard", "seq")),
        P(("shard", "seq")),
        P(("shard", "seq")),
        P(("shard", "seq")),
        P(("shard", "seq")),
    )
    out_specs = (
        P("shard", "seq", None),
        P("shard", "seq", None),
        P("shard", None),
        P(("shard", "seq"), None),
        P(("shard", "seq"), None),
        P(("shard", "seq"), None),
        P(("shard", "seq"), None),
        P(("shard", "seq"), None),
        P(("shard", "seq")),
        P(("shard", "seq")),
        P(("shard", "seq")),
        P(("shard", "seq")),
        P(("shard", "seq")),
    )
    return jax.shard_map(shards, mesh=mesh, in_specs=in_specs, out_specs=out_specs, check_vma=False)
```

```python
from functools import partial

import jax
import jax.numpy as jnp
from jax import lax
from jax.experimental import pallas as pl
from jax.experimental.pallas import tpu as pltpu
from jax.sharding import PartitionSpec as P

HD = 64


EPS = 1e-06

AXES = ("shard", "seq")

bf16 = jnp.bfloat16
f32 = jnp.float32


def modulate(tokens, shift_by, scale_by):
    average = jnp.mean(tokens, axis=-1, keepdims=True)
    centered = tokens - average
    variance = jnp.mean(centered * centered, axis=-1, keepdims=True)
    return centered * lax.rsqrt(variance + EPS) * (1.0 + scale_by) + shift_by


def cross_rows(left, right):
    return lax.dot_general(left, right, (((0,), (0,)), ((), ())), preferred_element_type=f32)


def along_cols(left, right):
    return lax.dot_general(left, right, (((1,), (1,)), ((), ())), preferred_element_type=f32)


def plain(left, right):
    return jnp.dot(left, right, preferred_element_type=f32)


LIMIT = 48 * 1024 * 1024


def call(kernel, flops, **kwargs):
    return pl.pallas_call(
        kernel,
        compiler_params=pltpu.CompilerParams(vmem_limit_bytes=LIMIT),
        cost_estimate=pl.CostEstimate(flops=flops // 50, bytes_accessed=flops // 10000, transcendentals=0),
        **kwargs,
    )


def transposed_dot(left, right):
    return lax.dot_general(left, right, (((1,), (1,)), ((), ())), preferred_element_type=f32)


def project_kernel(x_ref, *refs):
    parts, (bias_ref, out_ref) = refs[:-2], refs[-2:]
    weight = jnp.concatenate([part[...] for part in parts], axis=0)
    total = jnp.dot(x_ref[...], weight, preferred_element_type=f32)
    out_ref[...] = (total + bias_ref[...]).astype(out_ref.dtype)


def project(x, parts, begin, columns, bias, dtype):
    rows, depth = x.shape
    tile = 512
    first = begin // tile
    part_rows = depth // len(parts)
    return call(
        project_kernel,
        2 * rows * depth * columns,
        grid=(columns // tile,),
        in_specs=[pl.BlockSpec((rows, depth), lambda step: (0, 0))]
        + [pl.BlockSpec((part_rows, tile), lambda step: (0, first + step))] * len(parts)
        + [pl.BlockSpec((1, tile), lambda step: (0, step))],
        out_specs=pl.BlockSpec((rows, tile), lambda step: (0, step)),
        out_shape=jax.ShapeDtypeStruct((rows, columns), dtype),
    )(x, *parts, bias.reshape(1, -1))


def unproject_kernel(rows_ref, *refs):
    parts, out_ref = refs[:-1], refs[-1]
    weight = jnp.concatenate([part[...] for part in parts], axis=0)

    @pl.when(pl.program_id(0) == 0)
    def _():
        out_ref[...] = jnp.zeros(out_ref.shape, f32)

    out_ref[...] += transposed_dot(rows_ref[0], weight)


def unproject(rows, parts, first):
    blocks, count, width = rows.shape
    part_rows = width // len(parts)
    return call(
        unproject_kernel,
        2 * blocks * count * width * width,
        grid=(blocks,),
        in_specs=[pl.BlockSpec((1, count, width), lambda step: (step, 0, 0))]
        + [pl.BlockSpec((part_rows, width), lambda step: (0, first + step))] * len(parts),
        out_specs=pl.BlockSpec((count, width), lambda step: (0, 0)),
        out_shape=jax.ShapeDtypeStruct((count, width), f32),
    )(rows, *parts)


def attend_forward_kernel(q_ref, *refs):
    keys, values = refs[0:2], refs[2:4]
    out_ref, log_ref = refs[4:]
    count = q_ref.shape[0]
    outputs = []
    for head in range(2):
        cols = slice(head * HD, (head + 1) * HD)
        query = q_ref[:, cols] * jnp.bfloat16(HD ** (-0.5))
        scores = [transposed_dot(query, key[:, cols]) for key in keys]
        highest = jnp.maximum(
            jnp.max(scores[0], axis=1, keepdims=True), jnp.max(scores[1], axis=1, keepdims=True)
        )
        expon = [jnp.exp(score - highest) for score in scores]
        summed = jnp.sum(expon[0], axis=1, keepdims=True) + jnp.sum(expon[1], axis=1, keepdims=True)
        mixed = jnp.dot(expon[0].astype(bf16), values[0][:, cols], preferred_element_type=f32)
        mixed = mixed + jnp.dot(expon[1].astype(bf16), values[1][:, cols], preferred_element_type=f32)
        outputs.append(mixed / summed)
        logs = jnp.broadcast_to(highest + jnp.log(summed), (count, 128))
        log_ref[head] = jnp.transpose(logs)[0:1]
    out_ref[...] = jnp.concatenate(outputs, axis=1).astype(bf16)


def attend_forward(queries, keys, values):
    count, width = queries.shape
    pair = pl.BlockSpec((count, 2 * HD), lambda step: (0, step))
    steps = width // (2 * HD)
    return call(
        attend_forward_kernel,
        16 * count * count * width,
        grid=(steps,),
        in_specs=[pair] * 5,
        out_specs=[pair, pl.BlockSpec((2, 1, count), lambda step: (step, 0, 0))],
        out_shape=[
            jax.ShapeDtypeStruct((count, width), bf16),
            jax.ShapeDtypeStruct((2 * steps, 1, count), f32),
        ],
    )(queries, *keys, *values)


def attend_backward_kernel(q_ref, g_ref, log_ref, *refs):
    keys, values = refs[0:2], refs[2:4]
    own_ref, other_ref = refs[-2:]
    grads = [[], [], [], [], []]
    factor = HD ** (-0.5)
    for head in range(2):
        cols = slice(head * HD, (head + 1) * HD)
        query = q_ref[:, cols] * jnp.bfloat16(factor)
        grad = g_ref[:, cols]
        logs = log_ref[head]
        probs = [jnp.exp(transposed_dot(key[:, cols], query) - logs) for key in keys]
        grad_probs = [transposed_dot(value[:, cols], grad) for value in values]
        inner = jnp.sum(probs[0] * grad_probs[0], axis=0, keepdims=True)
        inner = inner + jnp.sum(probs[1] * grad_probs[1], axis=0, keepdims=True)
        grad_query = 0.0
        for side in range(2):
            grad_scores = (probs[side] * (grad_probs[side] - inner)).astype(bf16)
            grads[1 + 2 * side].append(jnp.dot(grad_scores, query, preferred_element_type=f32))
            grads[2 + 2 * side].append(
                jnp.dot(probs[side].astype(bf16), grad, preferred_element_type=f32)
            )
            grad_query = grad_query + cross_rows(grad_scores, keys[side][:, cols])
        grads[0].append(factor * grad_query)
    joined = [jnp.concatenate(part, axis=1).astype(bf16) for part in grads]
    for place in range(3):
        own_ref[place] = joined[place]
    for place in range(2):
        other_ref[place] = joined[3 + place]


def attend_backward(queries, grad_mixed, logs, keys, values, begin, steps, so_far):
    count, width = queries.shape
    pair = pl.BlockSpec((count, 2 * HD), lambda step: (0, begin + step))
    own = pl.BlockSpec((3, count, 2 * HD), lambda step: (0, 0, begin + step))
    other = pl.BlockSpec((2, count, 2 * HD), lambda step: (0, 0, begin + step))
    log_spec = pl.BlockSpec((2, 1, count), lambda step: (begin + step, 0, 0))
    operands = [queries, grad_mixed, logs, *keys, *values]
    specs = [pair, pair, log_spec] + [pair] * 4
    aliases = {}
    if so_far is not None:
        aliases = {len(operands): 0, len(operands) + 1: 1}
        operands = operands + list(so_far)
        specs = specs + [pl.BlockSpec(memory_space=pl.ANY)] * 2
    return call(
        attend_backward_kernel,
        40 * count * count * 2 * HD * steps,
        grid=(steps,),
        in_specs=specs,
        out_specs=[own, other],
        out_shape=[
            jax.ShapeDtypeStruct((3, count, width), bf16),
            jax.ShapeDtypeStruct((2, count, width), bf16),
        ],
        input_output_aliases=aliases,
    )(*operands)


def mlp_forward_kernel(x_ref, up_ref, down_ref, up_bias_ref, down_bias_ref, hidden_ref, slope_ref, out_ref):
    tile = hidden_ref.shape[1]
    pre = jnp.dot(x_ref[...], up_ref[...].reshape(-1, tile), preferred_element_type=f32)
    pre = pre + up_bias_ref[...]
    root, cubic = 0.7978845608028654, 0.044715
    square = pre * pre
    wave = jnp.tanh(root * pre * (1.0 + cubic * square))
    half = 0.5 * (1.0 + wave)
    slope = half + 0.5 * pre * (1.0 - wave * wave) * (root * (1.0 + 3.0 * cubic * square))
    slope_ref[...] = slope.astype(bf16)
    hidden = (pre * half).astype(bf16)
    hidden_ref[...] = hidden
    down = down_ref[...].reshape(tile, -1)

    @pl.when(pl.program_id(0) == 0)
    def _():
        out_ref[...] = jnp.broadcast_to(down_bias_ref[...], out_ref.shape)

    out_ref[...] += jnp.dot(hidden, down, preferred_element_type=f32)


def mlp_forward(x, mlp, up_bias, down_bias):
    count, width = x.shape
    hidden_width = up_bias.shape[0]
    tile = 512
    whole = pl.BlockSpec((count, width), lambda step: (0, 0))
    part = pl.BlockSpec((count, tile), lambda step: (0, step))
    return call(
        mlp_forward_kernel,
        4 * count * width * hidden_width,
        grid=(hidden_width // tile,),
        in_specs=[whole]
        + mlp.specs(tile)
        + [
            pl.BlockSpec((1, tile), lambda step: (0, step)),
            pl.BlockSpec((1, width), lambda step: (0, 0)),
        ],
        out_specs=[part, part, whole],
        out_shape=[
            jax.ShapeDtypeStruct((count, hidden_width), bf16),
            jax.ShapeDtypeStruct((count, hidden_width), bf16),
            jax.ShapeDtypeStruct((count, width), f32),
        ],
    )(x, *mlp.arrays, up_bias.reshape(1, -1), down_bias.reshape(1, -1))


def mlp_backward_kernel(grad_ref, up_ref, down_ref, slope_ref, grad_pre_ref, sums_ref, out_ref):
    tile = slope_ref.shape[1]
    grad_hidden = transposed_dot(grad_ref[...], down_ref[...].reshape(tile, -1))
    grad_pre = (grad_hidden * slope_ref[...].astype(f32)).astype(bf16)
    grad_pre_ref[...] = grad_pre
    sums_ref[...] = jnp.sum(grad_pre.astype(f32), axis=0, keepdims=True)

    @pl.when(pl.program_id(0) == 0)
    def _():
        out_ref[...] = jnp.zeros(out_ref.shape, f32)

    out_ref[...] += transposed_dot(grad_pre, up_ref[...].reshape(-1, tile))


def mlp_backward(grad, mlp, slope):
    count, width = grad.shape
    hidden_width = slope.shape[1]
    tile = 512
    whole = pl.BlockSpec((count, width), lambda step: (0, 0))
    part = pl.BlockSpec((count, tile), lambda step: (0, step))
    return call(
        mlp_backward_kernel,
        4 * count * width * hidden_width,
        grid=(hidden_width // tile,),
        in_specs=[whole] + mlp.specs(tile) + [part],
        out_specs=[part, pl.BlockSpec((1, tile), lambda step: (0, step)), whole],
        out_shape=[
            jax.ShapeDtypeStruct((count, hidden_width), bf16),
            jax.ShapeDtypeStruct((1, hidden_width), f32),
            jax.ShapeDtypeStruct((count, width), f32),
        ],
    )(grad, *mlp.arrays, slope)


class FeedForward:
    def __init__(self, up, down):
        self.rows_up, hidden_width = up.shape
        self.rows_down, self.width = down.shape
        cut_up = up.reshape(self.rows_up, -1, self.width).transpose(1, 0, 2).reshape(-1, self.width)
        both = lax.all_gather(jnp.concatenate([cut_up, down], axis=0), AXES, axis=0, tiled=False)
        self.in_place = self.rows_up % 16 == 0 and self.rows_down == cut_up.shape[0]
        if self.in_place:
            self.arrays = (both, both)
        else:
            devices = both.shape[0]
            up = both[:, : cut_up.shape[0]].reshape(devices, -1, self.rows_up, self.width)
            up = up.transpose(0, 2, 1, 3).reshape(1, devices * self.rows_up, hidden_width)
            down = both[:, cut_up.shape[0] :].reshape(1, hidden_width, self.width)
            self.arrays = (up, down)

    def specs(self, tile):
        up, down = self.arrays
        if not self.in_place:
            return [
                pl.BlockSpec((1, up.shape[1], tile), lambda step: (0, 0, step)),
                pl.BlockSpec((1, tile, self.width), lambda step: (0, step, 0)),
            ]
        across = self.width // tile
        return [
            pl.BlockSpec(
                (up.shape[0], self.rows_up, tile), lambda step: (0, step // across, step % across)
            ),
            pl.BlockSpec(
                (tile // self.rows_down, self.rows_down, self.width), lambda step: (step, 1, 0)
            ),
        ]


class Places:
    def __init__(self, latents):
        self.shards = lax.axis_size("shard")
        self.groups = lax.axis_size("seq")
        self.devices = self.shards * self.groups
        self.latents = latents
        assert 2 * latents == self.groups
        self.shard = lax.axis_index("shard")
        self.seq = lax.axis_index("seq")
        self.flat = self.shard * self.groups + self.seq
        self.core = self.shard % 2
        self.slot = self.seq % latents
        self.moves = []
        for turn in range(latents):
            move = []
            for source in range(self.devices):
                pair, core = divmod(source // self.groups, 2)
                half, place = divmod(source % self.groups, latents)
                member = (place + turn) % latents
                target = (2 * pair + half) * self.groups + core * latents + member
                move.append((source, target))
            self.moves.append(move)

    def to_pairs(self, blocks):
        parts = []
        for turn, move in enumerate(self.moves):
            member = (self.slot + turn) % self.latents
            block = lax.dynamic_index_in_dim(blocks, member, 0, keepdims=False)
            parts.append(lax.ppermute(block, AXES, move))
        return parts

    def from_pairs(self, rows):
        tokens = rows.shape[0] // self.latents
        parts = []
        for turn, move in enumerate(self.moves):
            block = rows[turn * tokens : (turn + 1) * tokens]
            parts.append(lax.ppermute(block, AXES, [(b, a) for a, b in move]))
        return parts

    def placed(self, parts):
        if len(parts) == 2:
            straight = self.slot == 0
            return jnp.stack(
                [jnp.where(straight, parts[0], parts[1]), jnp.where(straight, parts[1], parts[0])]
            )
        twice = jnp.stack(parts + parts)
        start = (self.latents - self.slot) % self.latents
        return lax.dynamic_slice_in_dim(twice, start, self.latents, axis=0)

    def across(self, array, mask=1):
        return lax.ppermute(array, "shard", [(s, s ^ mask) for s in range(self.shards)])

    def order(self):
        near = list(range(0, self.shards, 2))
        return near + [each ^ 1 for each in near]

    def arranged(self, matrix):
        width = matrix.shape[1] // self.shards
        return jnp.concatenate(
            [
                lax.dynamic_slice_in_dim(matrix, (self.shard ^ near) * width, width, axis=1)
                for near in self.order()
            ],
            axis=1,
        )

    def restored(self, matrix):
        width = matrix.shape[1] // self.shards
        order = self.order()
        places = jnp.array([order.index(near) for near in range(self.shards)], jnp.int32)
        return jnp.concatenate(
            [
                lax.dynamic_slice_in_dim(matrix, places[self.shard ^ s] * width, width, axis=1)
                for s in range(self.shards)
            ],
            axis=1,
        )

    def along_seq(self, block):
        parts = [block]
        for away in range(self.groups - 1, 0, -1):
            shift = [(q, (q + away) % self.groups) for q in range(self.groups)]
            parts.append(lax.ppermute(block, "seq", shift))
        start = ((self.groups - self.seq) % self.groups) * block.shape[0]
        twice = jnp.concatenate(parts + parts, axis=0)
        return lax.dynamic_slice_in_dim(twice, start, block.shape[0] * self.groups, axis=0)

    def gathered(self, block):
        parts = [block] + [self.across(block, mask) for mask in range(2, self.shards, 2)]
        return parts


class Reduction:
    def __init__(self, at, columns, right):
        self.at, self.columns, self.right = at, columns, right
        self.width = columns.shape[1] // at.shards
        self.received = []

    def piece(self, low, high):
        low, high = low * self.width, high * self.width
        left = self.columns[:, low:high]
        if self.right.ndim == 3:
            total = jnp.einsum("tm,ptn->pmn", left, self.right, preferred_element_type=f32)
        else:
            total = cross_rows(left, self.right)
        if self.received:
            total = total + self.received[0][..., low:high, :].astype(f32)
        return total

    def first(self):
        half = self.at.shards // 2
        return self.piece(half, 2 * half).astype(bf16)

    def send_first(self, block):
        self.received = [self.at.across(block)]

    def middle(self):
        return [self.piece(each, each + 1).astype(bf16) for each in range(1, self.at.shards // 2)]

    def send_middle(self, blocks):
        for each, block in enumerate(blocks):
            self.received.append(self.at.across(block, 2 * (each + 1)))

    def last(self):
        total = self.piece(0, 1)
        for part in self.received[1:]:
            total = total + part.astype(f32)
        return total.astype(bf16)

    def swap_last(self, block):
        groups = self.at.groups
        came = lax.all_to_all(block, "seq", 0, 0, tiled=True)
        return list(came.reshape(groups, -1, block.shape[1]))

    def split_last(self, total):
        at = self.at
        rows = self.width // at.groups

        def block(away):
            begin = ((at.seq + away) % at.groups) * rows
            return lax.dynamic_slice_in_dim(total, begin, rows, axis=total.ndim - 2)

        return [block(away) for away in range(at.groups)]

    def send_last(self, blocks):
        at = self.at
        came = []
        for away in range(1, at.groups):
            shift = [(q, (q + away) % at.groups) for q in range(at.groups)]
            came.append(lax.ppermute(blocks[away], "seq", shift))
        return blocks[:1] + came


def total_of(blocks):
    total = blocks[0].astype(f32)
    for block in blocks[1:]:
        total = total + block.astype(f32)
    return total


def tied(*arrays):
    return lax.optimization_barrier(arrays)


def shards(
    hidden_in,
    condition,
    out_grad,
    ada_weight,
    qkv_weight,
    proj_weight,
    up_weight,
    down_weight,
    ada_bias,
    qv_bias,
    proj_bias,
    up_bias,
    down_bias,
):
    latents, local_len, width = hidden_in.shape
    at = Places(latents)
    pairs = at.shards // 2
    total_latents = pairs * at.groups
    depth = ada_weight.shape[0]

    mlp = FeedForward(up_weight, down_weight)
    near_rows = at.along_seq(jnp.concatenate([qkv_weight, proj_weight], axis=1))

    silu_rows = jax.nn.silu(condition.astype(f32)).astype(bf16)
    silu_rows = silu_rows.reshape(latents, at.shards, at.groups, depth)
    silu_rows = lax.dynamic_index_in_dim(silu_rows, at.seq, 2, keepdims=False)
    silu_rows = silu_rows.transpose(1, 0, 2).reshape(at.shards, latents * depth)
    silu_rows = lax.all_to_all(silu_rows, "shard", 0, 0, tiled=True).reshape(total_latents, depth)
    share = plain(silu_rows, ada_weight)
    wide = share.shape[1]
    share = share.reshape(pairs, at.groups, 2, wide // 2).transpose(0, 2, 1, 3)
    share = share.reshape(at.devices, wide // 2)
    biases = jnp.concatenate([ada_bias, qv_bias, proj_bias, up_bias, down_bias]).astype(f32)
    cuts = [ada_bias.shape[0], qv_bias.shape[0], proj_bias.shape[0], up_bias.shape[0], down_bias.shape[0]]
    sent = jnp.concatenate([share, jnp.broadcast_to(biases, (at.devices, biases.shape[0]))], axis=1)
    sent, near_rows, hidden_in = tied(sent, near_rows, hidden_in)
    came = lax.all_to_all(sent, AXES, 0, 0, tiled=True)
    near_parts = at.gathered(near_rows)
    tokens = at.to_pairs(hidden_in)
    came, *tokens = tied(came, *tokens)
    mine = jnp.sum(came[:, : wide // 2], axis=0)
    other = at.across(mine)
    modulation = jnp.where(
        at.core == 0, jnp.concatenate([mine, other]), jnp.concatenate([other, mine])
    )
    whole = []
    begin = wide // 2
    for cut in cuts:
        whole.append(came[:, begin : begin + cut].reshape(-1))
        begin += cut
    b_ada, b_qv, b_proj, b_up, b_down = whole
    modulation = (modulation + b_ada).reshape(6, width)
    shift_a, scale_a, gate_a, shift_m, scale_m, gate_m = [modulation[member] for member in range(6)]

    tokens = jnp.concatenate(tokens, axis=0).astype(f32)
    normed = modulate(tokens, shift_a, scale_a).astype(bf16)
    normed_cols = at.arranged(normed)
    normed_cols, *near_parts = tied(normed_cols, *near_parts)
    weight = near_parts + [at.across(part) for part in near_parts]
    key_own = project(normed_cols, weight, width, width, jnp.zeros((width,), f32), bf16)
    keys = (key_own, at.across(key_own))
    value_own = project(normed_cols, weight, 2 * width, width, b_qv[width:], bf16)
    values = (value_own, at.across(value_own))
    queries = project(normed_cols, weight, 0, width, b_qv[:width], bf16)
    queries, out_grad = tied(queries, out_grad)
    cotangent = at.to_pairs(out_grad)
    mixed, logs = attend_forward(queries, keys, values)
    mixed_cols = at.arranged(mixed)
    attn_out = project(mixed_cols, weight, 3 * width, width, b_proj, f32)
    middle = tokens + gate_a * attn_out
    normed_two = modulate(middle, shift_m, scale_m).astype(bf16)
    hidden, slope, mlp_out = mlp_forward(normed_two, mlp, b_up, b_down)
    hidden, *cotangent = tied(hidden, *cotangent)
    block_rows = (middle + gate_m * mlp_out).astype(bf16)

    cotangent = jnp.concatenate(cotangent, axis=0).astype(f32)
    grad_gate_m = jnp.sum(cotangent * mlp_out, axis=0)
    grad_mlp = (gate_m * cotangent).astype(bf16)
    grad_bdown = jnp.sum(grad_mlp.astype(f32), axis=0)
    down_sum = Reduction(at, at.arranged(hidden), grad_mlp)
    slope, block, block_rows = tied(slope, down_sum.first(), block_rows)
    down_sum.send_first(block)
    block_out = at.from_pairs(block_rows)
    grad_pre, grad_bup, grad_normed_two = mlp_backward(grad_mlp, mlp, slope)
    grad_pre, grad_normed_two, *down_sum.received = tied(
        grad_pre, grad_normed_two, *down_sum.received
    )
    up_sum = Reduction(at, at.arranged(normed_two), grad_pre)
    grad_normed_two, block, *blocks = tied(grad_normed_two, up_sum.first(), *down_sum.middle())
    down_sum.send_middle(blocks)
    up_sum.send_first(block)
    _, second_back = jax.vjp(modulate, middle, shift_m, scale_m)
    grad_middle, grad_shift_m, grad_scale_m = second_back(grad_normed_two)
    grad_middle = grad_middle + cotangent

    grad_gate_a = jnp.sum(grad_middle * attn_out, axis=0)
    grad_attn = (gate_a * grad_middle).astype(bf16)
    grad_bproj = jnp.sum(grad_attn.astype(f32), axis=0)
    grad_mixed = at.restored(unproject(grad_attn[None], weight, 3).astype(bf16))
    proj_sum = Reduction(at, mixed_cols, grad_attn)
    grad_mixed, *up_sum.received = tied(grad_mixed, *up_sum.received)
    grad_mixed, block, *blocks = tied(grad_mixed, proj_sum.first(), *up_sum.middle())
    up_sum.send_middle(blocks)
    proj_sum.send_first(block)
    head_pairs = width // (2 * HD)
    cut = head_pairs // 2
    grads = attend_backward(queries, grad_mixed, logs, keys, values, 0, cut, None)
    *grads, proj_sum.received, down_sum.received, block_out = tied(
        *grads, proj_sum.received, down_sum.received, block_out
    )
    *grads, block = tied(*grads, down_sum.last())
    down_came = down_sum.swap_last(block)
    own_grads, other_grads = attend_backward(
        queries, grad_mixed, logs, keys, values, cut, head_pairs - cut, grads
    )
    own_grads, other_grads, down_came, up_sum.received = tied(
        own_grads, other_grads, down_came, up_sum.received
    )
    other_grads, up_block, *blocks = tied(other_grads, up_sum.last(), *proj_sum.middle())
    kv_came = at.across(other_grads)
    up_came = up_sum.swap_last(up_block)
    proj_sum.send_middle(blocks)
    grad_rows = jnp.concatenate([own_grads[:1], own_grads[1:] + kv_came], axis=0)
    qkv_sum = Reduction(at, normed_cols, grad_rows)
    grad_rows, block = tied(grad_rows, qkv_sum.first())
    qkv_sum.send_first(block)
    down_share = total_of(down_came)
    column_sums = jnp.sum(grad_rows.astype(f32), axis=1)
    grad_bqv = jnp.concatenate([column_sums[0], column_sums[2]])
    grad_normed = unproject(grad_rows, weight, 0)
    grad_normed, qkv_sum.received, proj_sum.received = tied(
        grad_normed, qkv_sum.received, proj_sum.received
    )
    grad_normed, block, *blocks = tied(grad_normed, proj_sum.last(), *qkv_sum.middle())
    qkv_sum.send_middle(blocks)
    proj_came = proj_sum.swap_last(block)
    grad_normed = at.restored(grad_normed)
    _, first_back = jax.vjp(modulate, tokens, shift_a, scale_a)
    grad_tokens, grad_shift_a, grad_scale_a = first_back(grad_normed)
    hidden_rows = (grad_tokens + grad_middle).astype(bf16)

    part_mod = jnp.concatenate(
        [grad_shift_a, grad_scale_a, grad_gate_a, grad_shift_m, grad_scale_m, grad_gate_m]
    )
    part_mod, hidden_rows, up_came = tied(part_mod, hidden_rows, up_came)
    mod_came = at.across(part_mod)
    hidden_grad = at.from_pairs(hidden_rows)
    grad_mod = (part_mod + mod_came).astype(bf16)
    half_mod = lax.dynamic_slice_in_dim(grad_mod, at.core * (wide // 2), wide // 2).astype(f32)
    bias_parts = [
        part.reshape(at.devices, -1) for part in (grad_bqv, grad_bproj, grad_bup, grad_bdown)
    ]
    sent = jnp.concatenate(
        [jnp.broadcast_to(half_mod, (at.devices, wide // 2))] + bias_parts, axis=1
    )
    came = lax.all_to_all(sent, AXES, 0, 0, tiled=True)
    came, proj_came, hidden_grad, qkv_sum.received = tied(
        came, proj_came, hidden_grad, qkv_sum.received
    )
    came, block = tied(came, qkv_sum.last())
    qkv_came = qkv_sum.send_last(qkv_sum.split_last(block))
    up_share, proj_share = total_of(up_came), total_of(proj_came)
    every_mod = came[:, : wide // 2].reshape(pairs, 2, at.groups, wide // 2)
    every_mod = every_mod.transpose(0, 2, 1, 3).reshape(total_latents, wide).astype(bf16)
    bias_sums = jnp.sum(came[:, wide // 2 :], axis=0)
    bias_shares = []
    begin = 0
    for part in bias_parts:
        bias_shares.append(bias_sums[begin : begin + part.shape[1]])
        begin += part.shape[1]
    ada_share = cross_rows(silu_rows, every_mod)
    own_bias = ada_bias.shape[0]
    adabias_share = jnp.sum(
        lax.dynamic_slice_in_dim(every_mod, at.flat * own_bias, own_bias, axis=1).astype(f32), axis=0
    )
    grad_silu = along_cols(every_mod, ada_weight).reshape(at.shards, 1, latents * depth)
    sent = jnp.broadcast_to(grad_silu, (at.shards, at.groups, latents * depth))
    came = lax.all_to_all(sent.reshape(at.devices, latents * depth), AXES, 0, 0, tiled=True)
    grad_silu = came.reshape(at.devices, latents, depth).transpose(1, 0, 2).reshape(latents, width)
    _, silu_back = jax.vjp(jax.nn.silu, condition.astype(f32))
    condition_grad = silu_back(grad_silu)[0]
    qkv_share = total_of(qkv_came).transpose(1, 0, 2).reshape(-1, 3 * width)
    return (
        at.placed(block_out),
        at.placed(hidden_grad).astype(f32),
        condition_grad,
        ada_share,
        qkv_share,
        proj_share,
        up_share,
        down_share,
        adabias_share,
        bias_shares[0],
        bias_shares[1],
        bias_shares[2],
        bias_shares[3],
    )


def solution(mesh):
    in_specs = (
        P("shard", "seq", None),
        P("shard", None),
        P("shard", "seq", None),
        P(("shard", "seq"), None),
        P(("shard", "seq"), None),
        P(("shard", "seq"), None),
        P(("shard", "seq"), None),
        P(("shard", "seq"), None),
        P(("shard", "seq")),
        P(("shard", "seq")),
        P(("shard", "seq")),
        P(("shard", "seq")),
        P(("shard", "seq")),
    )
    out_specs = (
        P("shard", "seq", None),
        P("shard", "seq", None),
        P("shard", None),
        P(("shard", "seq"), None),
        P(("shard", "seq"), None),
        P(("shard", "seq"), None),
        P(("shard", "seq"), None),
        P(("shard", "seq"), None),
        P(("shard", "seq")),
        P(("shard", "seq")),
        P(("shard", "seq")),
        P(("shard", "seq")),
        P(("shard", "seq")),
    )
    return jax.shard_map(shards, mesh=mesh, in_specs=in_specs, out_specs=out_specs, check_vma=False)
```
